512 devices in a mesh: context: 32 (over z, core), fheads: 4 (over x), seqs: 4 (over y).
Axes of the slice: x: 4, y: 4, z: 16, core: 2. Of those that a mesh axis runs over, the one named last changes fastest.
Arguments:
- query_rows: bfloat16 [65536, 3072], P(('seqs', 'context'), 'fheads'), parts along dimension 0, may hold values from -5 to 5
- key_rows: bfloat16 [65536, 3072], P(('seqs', 'context'), 'fheads'), parts along dimension 0, may hold values from -5 to 5
- value_rows: bfloat16 [65536, 3072], P(('seqs', 'context'), 'fheads'), parts along dimension 0, may hold values from -10 to 10
- step_sizes: float32 [65536, 4], P(('seqs', 'context'), 'fheads'), parts along dimension 0, may hold values from 2e-05 to 0.0018
- w_gate: bfloat16 [4, 768, 768], P('fheads', 'context'), may hold values from -4 to 4
- w_up: bfloat16 [4, 768, 768], P('fheads', 'context'), may hold values from -4 to 4
- w_down: bfloat16 [4, 768, 768], P('fheads', 'context'), may hold values from -4 to 4
Outputs:
- window_out: bfloat16 [65536, 3072], P(('seqs', 'context'), 'fheads'), parts along dimension 0
- fast_out: bfloat16 [65536, 3072], P(('seqs', 'context'), 'fheads'), parts along dimension 0
The draws below stay inside these ranges and needn't reach their ends.
There are 4 independent parts, one for each index of `seqs`. The reference program is written for one: setup_inputs(seed, part) draws one part's arguments, and reference() takes and returns one part's arrays. A program takes and returns all parts, laid end to end along the dimension named above; an argument that names none is the same for every part. Nothing has to cross between parts.
All inputs are finite; a program needn't handle non-finite values.
Results may differ from the reference program's by a relative error of at most 0.035.
Values may be sent and summed in bfloat16 or wider, within the bound.
A program may use at most 128 MiB of HBM per device.

```python
import math
import jax
import jax.numpy as jnp
from jax import lax

D = 3072
HEADS = 24
HD = 128
FHEADS = 4
FD = 768
WINDOW = 512
TOK_DEV = 512
LENGTH = 16384
N_CONTEXT = 32


def paired_fields(base):
    first_key = jax.random.fold_in(base, 11)
    second_key = jax.random.fold_in(base, 12)
    limit_value = 5.0 / 1.5
    queries = 1.5 * jax.random.truncated_normal(first_key, -limit_value, limit_value, (LENGTH, D), jnp.float32)
    keys_drawn = 1.5 * jax.random.truncated_normal(second_key, -limit_value, limit_value, (LENGTH, D), jnp.float32)
    return (queries, keys_drawn)


def draw_query_rows(key, part):
    return paired_fields(key)[0].astype(jnp.bfloat16)


def draw_key_rows(key, part):
    return paired_fields(key)[1].astype(jnp.bfloat16)


def draw_step_sizes(key, part):
    position = jnp.arange(LENGTH, dtype=jnp.float32) / max(LENGTH - 1, 1)
    ramp_top = 3.0
    base_rate = jnp.exp(jax.random.uniform(key, (LENGTH, FHEADS), jnp.float32, math.log(2e-05), math.log(0.0002)))
    return base_rate * (ramp_top ** position)[:, None]


def fast_matrix(base, salt, gain):
    salted = jax.random.fold_in(base, salt)
    row_key = jax.random.fold_in(salted, 1)
    column_key = jax.random.fold_in(salted, 2)
    entry_key = jax.random.fold_in(salted, 3)
    spread = 10.0
    ramp_top = 3.0
    ramp = ramp_top ** (jnp.arange(FD, dtype=jnp.float32) / max(FD - 1, 1))
    row_scale = jnp.exp(jax.random.uniform(row_key, (FHEADS, FD, 1), jnp.float32, 0.0, math.log(spread))) * ramp[None, :, None]
    row_scale = row_scale / jnp.sqrt(jnp.sum(row_scale * row_scale, axis=1, keepdims=True))
    column_scale = jnp.exp(jax.random.uniform(column_key, (FHEADS, 1, FD), jnp.float32, 0.0, math.log(spread)))
    column_scale = column_scale / jnp.sqrt(jnp.mean(column_scale * column_scale, axis=2, keepdims=True))
    entries = jax.random.truncated_normal(entry_key, -4.0, 4.0, (FHEADS, FD, FD), jnp.float32)
    return jnp.clip(gain * entries * row_scale * column_scale, -4.0, 4.0)


def draw_w_gate(key, part):
    return fast_matrix(key, 21, 1.0).astype(jnp.bfloat16)


def draw_w_up(key, part):
    return fast_matrix(key, 22, 1.0).astype(jnp.bfloat16)


def draw_w_down(key, part):
    return fast_matrix(key, 23, 2.0).astype(jnp.bfloat16)


def block_scale(rng, shape, split, least, top_value):
    level, own = 1.0, jax.random.fold_in(rng, 6)
    for dim, parts in split:
        heights = jnp.exp(jax.random.uniform(jax.random.fold_in(own, dim), (parts,), jnp.float32, least / len(split), top_value / len(split)))
        level = level * jnp.repeat(heights, shape[dim] // parts).reshape([-1 if axis == dim else 1 for axis in range(len(shape))])
    return level


def scatter_about(key, dims, deviation, limit, pieces=(), held_as=jnp.bfloat16):
    level = block_scale(key, dims, pieces, -0.22, 0.18) if pieces else 1.0
    array = jax.random.normal(key, dims, jnp.float32) * deviation * level
    return jnp.minimum(jnp.maximum(array, -limit), limit).astype(held_as)


def setup_inputs(seed: int = 0, part: int = 0) -> dict:
    key_of = jax.random.split(jax.random.key(seed), 8)
    part_keys = jax.random.split(jax.random.fold_in(key_of[7], part), 8)
    return {
        "query_rows": draw_query_rows(jax.random.fold_in(jax.random.fold_in(key_of[7], part), 71), part),
        "key_rows": draw_key_rows(jax.random.fold_in(jax.random.fold_in(key_of[7], part), 71), part),
        "value_rows": scatter_about(part_keys[2], (LENGTH, D), 2.0, 10.0, ((0, 32), (1, 4))),
        "step_sizes": draw_step_sizes(jax.random.fold_in(jax.random.fold_in(key_of[7], part), 71), part),
        "w_gate": draw_w_gate(jax.random.fold_in(key_of[7], 71), part),
        "w_up": draw_w_up(jax.random.fold_in(key_of[7], 71), part),
        "w_down": draw_w_down(jax.random.fold_in(key_of[7], 71), part),
    }


def unit_rows(values):
    return values * lax.rsqrt(lax.optimization_barrier(jnp.mean(values * values, axis=-1, keepdims=True)) + 1e-06)

def window_block(queries, keys_near, values_near, first_pos):
    row_count = queries.shape[0]
    query_pos = first_pos + jnp.arange(row_count, dtype=jnp.int32)
    key_pos = first_pos - WINDOW + jnp.arange(row_count + WINDOW, dtype=jnp.int32)
    allowed = (key_pos[None, :] >= 0) & (key_pos[None, :] <= query_pos[:, None]) & (key_pos[None, :] > query_pos[:, None] - WINDOW)
    scores = jnp.einsum('ihd,jhd->hij', queries.astype(jnp.float32), keys_near.astype(jnp.float32)) / math.sqrt(HD)
    scores = jnp.where(allowed[None], scores, -1e+30)
    row_max = lax.optimization_barrier(jnp.max(scores, axis=-1, keepdims=True))
    powers = jnp.exp(scores - row_max)
    weights = (powers / lax.optimization_barrier(jnp.sum(powers, axis=-1, keepdims=True))).astype(jnp.bfloat16)
    attended = jnp.einsum('hij,jhd->ihd', weights.astype(jnp.float32), values_near.astype(jnp.float32))
    return attended.astype(jnp.bfloat16)

def attention(query_rows, key_rows, value_rows):
    queries = query_rows.reshape(LENGTH, HEADS, HD)
    padding = jnp.zeros((WINDOW, HEADS, HD), key_rows.dtype)
    keys_padded = jnp.concatenate([padding, key_rows.reshape(LENGTH, HEADS, HD)], axis=0)
    values_padded = jnp.concatenate([padding, value_rows.reshape(LENGTH, HEADS, HD)], axis=0)

    def one_block(block_index):
        first_row = block_index * TOK_DEV
        return window_block(lax.dynamic_slice_in_dim(queries, first_row, TOK_DEV, 0), lax.dynamic_slice_in_dim(keys_padded, first_row, TOK_DEV + WINDOW, 0), lax.dynamic_slice_in_dim(values_padded, first_row, TOK_DEV + WINDOW, 0), first_row)
    blocks = lax.map(one_block, jnp.arange(N_CONTEXT, dtype=jnp.int32))
    return blocks.reshape(LENGTH, HEADS * HD)

def dot_rows(first_op, second_op):
    return lax.dot_general(first_op, second_op, (((0,), (0,)), ((), ())), preferred_element_type=jnp.float32)

def dot_back(first_op, second_op):
    return lax.dot_general(first_op, second_op, (((1,), (1,)), ((), ())), preferred_element_type=jnp.float32)

def renormed(weight, gradient):
    initial = weight.astype(jnp.float32)
    fresh_rows = initial - gradient
    old_ms = lax.optimization_barrier(jnp.mean(initial * initial, axis=0))
    new_ms = lax.optimization_barrier(jnp.mean(fresh_rows * fresh_rows, axis=0))
    return (fresh_rows * jnp.sqrt(old_ms) * lax.rsqrt(new_ms + 1e-06)).astype(jnp.bfloat16)

def apply_fast(fast_queries, gate_w, up_w, down_w):
    gate_new = jnp.dot(fast_queries, gate_w, preferred_element_type=jnp.float32)
    up_new = jnp.dot(fast_queries, up_w, preferred_element_type=jnp.float32)
    hidden_new = (gate_new * jax.nn.sigmoid(gate_new) * up_new).astype(jnp.bfloat16)
    return jnp.dot(hidden_new, down_w, preferred_element_type=jnp.float32).astype(jnp.bfloat16)

def fast_head(queries, keys_in, values_in, step_sizes, gate_w, up_w, down_w):
    fast_keys = unit_rows(keys_in.astype(jnp.float32)).astype(jnp.bfloat16)
    fast_queries = unit_rows(queries.astype(jnp.float32)).astype(jnp.bfloat16)
    target = (-(step_sizes * values_in.astype(jnp.float32))).astype(jnp.bfloat16)
    gate_pre = jnp.dot(fast_keys, gate_w, preferred_element_type=jnp.float32)
    up_pre = jnp.dot(fast_keys, up_w, preferred_element_type=jnp.float32)
    sigmoid_gate = jax.nn.sigmoid(gate_pre)
    hidden = (gate_pre * sigmoid_gate * up_pre).astype(jnp.bfloat16)
    back_grad = dot_back(target, down_w)
    d_gate = (back_grad * up_pre * sigmoid_gate * (1.0 + gate_pre * (1.0 - sigmoid_gate))).astype(jnp.bfloat16)
    d_up = (back_grad * gate_pre * sigmoid_gate).astype(jnp.bfloat16)

    def accumulate(totals, block_index):
        first_row = block_index * TOK_DEV
        keys_block = lax.dynamic_slice_in_dim(fast_keys, first_row, TOK_DEV, 0)
        hidden_block = lax.dynamic_slice_in_dim(hidden, first_row, TOK_DEV, 0)
        target_block = lax.dynamic_slice_in_dim(target, first_row, TOK_DEV, 0)
        gate_block = lax.dynamic_slice_in_dim(d_gate, first_row, TOK_DEV, 0)
        up_block = lax.dynamic_slice_in_dim(d_up, first_row, TOK_DEV, 0)
        partials = (dot_rows(keys_block, gate_block), dot_rows(keys_block, up_block), dot_rows(hidden_block, target_block))
        rounded = tuple((lax.optimization_barrier(term.astype(jnp.bfloat16)).astype(jnp.float32) for term in partials))
        return (tuple((totals[number] + rounded[number] for number in range(3))), None)
    empty = jnp.zeros((FD, FD), jnp.float32)
    sums, _ = lax.scan(accumulate, (empty, empty, empty), jnp.arange(N_CONTEXT, dtype=jnp.int32))
    updated_gate = renormed(gate_w, sums[0])
    updated_up = renormed(up_w, sums[1])
    updated_down = renormed(down_w, sums[2])
    return apply_fast(fast_queries, updated_gate, updated_up, updated_down)

def reference(query_rows, key_rows, value_rows, step_sizes, w_gate, w_up, w_down):
    window_out = attention(query_rows, key_rows, value_rows)
    outputs = []
    for head_number in range(FHEADS):
        columns = slice(head_number * FD, (head_number + 1) * FD)
        outputs.append(fast_head(query_rows[:, columns], key_rows[:, columns], value_rows[:, columns], step_sizes[:, head_number:head_number + 1], w_gate[head_number], w_up[head_number], w_down[head_number]))
    return (window_out, jnp.concatenate(outputs, axis=1))
```

```python
import functools
import math

import jax
import jax.numpy as jnp
from jax import lax
from jax.experimental import pallas as pl
from jax.experimental.pallas import tpu as pltpu
from jax.sharding import PartitionSpec as P

MESH = pl.DeviceIdType.MESH
F32 = jnp.float32
BF16 = jnp.bfloat16
HD = 128
WINDOW = 512
NZ = 16
TOK = 512
FD = 768
SLAB = FD // NZ
HALF = FD // 2
SENDS = ((8, 7), (7, 8), (8, 7))
NN = (((1,), (0,)), ((), ()))
NT = (((1,), (1,)), ((), ()))
TN = (((0,), (0,)), ((), ()))


def dot(a, b, dims):
    return lax.dot_general(a, b, dims, preferred_element_type=F32)


def kernel(
    q_in, k_in, v_in, step_ref, wg_ref, wu_ref, wd_ref, wout, fout,
    qs, kcat, vcat, fk, fq, tgt, wpad, wsib, w_all, grad, grad_sib, run, w_t, fresh, sq_mine, sq_sib, u_all, hid,
    in_sem, halo_send, halo_recv, pad_send, pad_recv, a_send, a_recv, ad_send, ad_recv,
    g_send, g_recv, r_send, r_recv, q_send, q_recv, u_send, u_recv, ud_send, ud_recv,
):
    c = lax.axis_index("context")
    core = lax.rem(c, 2)
    z = lax.div(c, 2)
    n = 2 * NZ
    sib = c + 1 - 2 * core
    nxt = (lax.rem(c + 2, n), lax.rem(c + n - 2, n))
    following = lax.rem(c + 1, n)

    def around(k):
        return lax.rem(z + k + 2 * NZ, NZ)

    def rows(slab):
        return pl.ds(pl.multiple_of(slab * SLAB, 16), SLAB)

    mine = pl.ds(pl.multiple_of(core * HALF, 128), HALF)
    other = pl.ds(pl.multiple_of((1 - core) * HALF, 128), HALF)

    def remote(src, dst, send, recv, to):
        return pltpu.make_async_remote_copy(
            src_ref=src, dst_ref=dst, send_sem=send, recv_sem=recv,
            device_id={"context": to}, device_id_type=MESH,
        )

    loads = (
        pltpu.make_async_copy(k_in, kcat.at[pl.ds(WINDOW, TOK)], in_sem.at[0]),
        pltpu.make_async_copy(v_in, vcat.at[pl.ds(WINDOW, TOK)], in_sem.at[1]),
        pltpu.make_async_copy(q_in, qs, in_sem.at[2]),
    )
    for load in loads:
        load.start()

    barrier = pltpu.get_barrier_semaphore()
    for step in (1, 2, n - 1, n - 2):
        pl.semaphore_signal(
            barrier, inc=1, device_id={"context": lax.rem(c + step, n)}, device_id_type=MESH
        )
    for m, ref in enumerate((wg_ref, wu_ref, wd_ref)):
        block = ref[0].astype(F32)
        wpad[m] = jnp.concatenate([block, jnp.zeros((8, FD), F32)], axis=0).astype(BF16)
    pl.semaphore_wait(barrier, 4)

    pad = remote(wpad, wsib, pad_send, pad_recv, sib)
    pad.start()
    pad.wait()
    for m in range(3):
        own = wpad[m].astype(F32)[:24]
        sibs = wsib[m].astype(F32)[:24]
        low = jnp.where(core == 0, own, sibs)
        high = jnp.where(core == 0, sibs, own)
        w_all[m, rows(z), :] = jnp.concatenate([low, high], axis=0).astype(BF16)

    def ring_gather(buf, z_send, z_recv, d_send, d_recv, filler):
        def z_copy(d, m, s):
            slab = around(-s) if d == 0 else around(s)
            view = buf.at[m, rows(slab), mine]
            return remote(view, view, z_send.at[d, m, s], z_recv.at[d, m, s], nxt[d])

        def d_copy(d, m, s):
            slab = around(-s) if d == 0 else around(s)
            view = buf.at[m, rows(slab), mine]
            return remote(view, view, d_send.at[d, m, s], d_recv.at[d, m, s], sib)

        for m in range(3):
            for d in range(2):
                z_copy(d, m, 0).start()
        filler(0)

        def turn(s, carry):
            for m in range(3):
                for d in range(2):
                    z_copy(d, m, s - 1).wait_recv()
                    z_copy(d, m, s).start()
                    d_copy(d, m, s).start()
            filler(s)
            return carry

        lax.fori_loop(1, 7, turn, 0)
        for m in range(3):
            for d in range(2):
                z_copy(d, m, 6).wait_recv()
                if SENDS[m][d] == 8:
                    z_copy(d, m, 7).start()
                d_copy(d, m, 7).start()
        for m in range(3):
            for d in range(2):
                if SENDS[m][d] == 8:
                    z_copy(d, m, 7).wait_recv()
                    d_copy(d, m, 8).start()

        def settle(s, carry):
            for m in range(3):
                for d in range(2):
                    z_copy(d, m, s - 1).wait_send()
                    d_copy(d, m, s).wait()
            return carry

        lax.fori_loop(1, 8, settle, 0)
        for m in range(3):
            for d in range(2):
                if SENDS[m][d] == 8:
                    z_copy(d, m, 7).wait_send()
                    d_copy(d, m, 8).wait()

    halo = (
        remote(kcat.at[pl.ds(WINDOW, TOK)], kcat.at[pl.ds(0, WINDOW)], halo_send.at[0], halo_recv.at[0], following),
        remote(vcat.at[pl.ds(WINDOW, TOK)], vcat.at[pl.ds(0, WINDOW)], halo_send.at[1], halo_recv.at[1], following),
    )

    def prepare(b):
        r = pl.ds(pl.multiple_of(b * 64, 64), 64)
        near = pl.ds(pl.multiple_of(b * 64 + WINDOW, 64), 64)
        k = kcat[near, :].astype(F32)
        fk[r, :] = (k * lax.rsqrt(jnp.mean(k * k, axis=-1, keepdims=True) + 1e-06)).astype(BF16)
        x = qs[r, :].astype(F32)
        fq[r, :] = (x * lax.rsqrt(jnp.mean(x * x, axis=-1, keepdims=True) + 1e-06)).astype(BF16)
        tgt[r, :] = (-(step_ref[r, :] * vcat[near, :].astype(F32))).astype(BF16)

    def gather_filler(s):
        if isinstance(s, int):
            for load in loads:
                load.wait()

            def body(b, carry):
                prepare(b)
                return carry

            lax.fori_loop(0, 8, body, 0)

    ring_gather(w_all, a_send, a_recv, ad_send, ad_recv, gather_filler)
    for copy in halo:
        copy.start()

    def hidden_block(b, carry):
        cols = pl.ds(pl.multiple_of(b * 256, 256), 256)
        gate = dot(fk[...], w_all[0, :, cols], NN)
        up = dot(fk[...], w_all[1, :, cols], NN)
        sg = jax.nn.sigmoid(gate)
        hidden = (gate * sg * up).astype(BF16)
        back = dot(tgt[...], w_all[2, cols, :], NT)
        d_gate = (back * up * sg * (1.0 + gate * (1.0 - sg))).astype(BF16)
        d_up = (back * gate * sg).astype(BF16)
        grad[0, cols, :] = dot(d_gate, fk[...], TN).astype(BF16)
        grad[1, cols, :] = dot(d_up, fk[...], TN).astype(BF16)
        grad[2, :, cols] = dot(tgt[...], hidden, TN).astype(BF16)
        return carry

    lax.fori_loop(0, 3, hidden_block, 0)

    def g_copy(m):
        return remote(grad.at[m, :, other], grad_sib.at[m], g_send.at[m], g_recv.at[m], sib)

    for m in range(3):
        g_copy(m).start()

    pick = (
        lax.broadcasted_iota(jnp.int32, (SLAB, FD), 1)
        == lax.broadcasted_iota(jnp.int32, (SLAB, FD), 0) + z * SLAB
    ).astype(BF16)
    for m in range(3):
        w_t[m] = dot(pick, w_all[m], NT)

    for m in range(3):
        g_copy(m).wait_recv()
    for copy in halo:
        copy.wait_recv()

    def local(m, slab):
        return grad[m, rows(slab), mine].astype(F32) + grad_sib[m, rows(slab), :].astype(F32)

    def r_copy(d, m, s):
        return remote(run.at[d, m, s], run.at[d, m, s + 1], r_send.at[d, m, s], r_recv.at[d, m, s], nxt[d])

    def r_slab(d, m, s):
        return around(SENDS[m][0] - s) if d == 0 else around(s - SENDS[m][1])

    low_limit = jnp.where(c == 0, WINDOW, 0)

    def attend(piece):
        h = lax.div(piece, 4)
        first = pl.multiple_of(lax.rem(piece, 4) * 128, 128)
        cols = pl.ds(pl.multiple_of(h * HD, HD), HD)
        kb = kcat[pl.ds(first, 640), cols]
        vb = vcat[pl.ds(first, 640), cols]
        scores = dot(qs[pl.ds(first, 128), cols], kb, NT) * (1.0 / math.sqrt(HD))
        t = lax.broadcasted_iota(jnp.int32, (128, 640), 0)
        j = lax.broadcasted_iota(jnp.int32, (128, 640), 1)
        allowed = (j > t) & (j <= t + WINDOW) & (j + first >= low_limit)
        scores = jnp.where(allowed, scores, -1e30)
        powers = jnp.exp(scores - jnp.max(scores, axis=-1, keepdims=True))
        total = jnp.sum(powers, axis=-1, keepdims=True)
        wout[pl.ds(first, 128), cols] = (dot(powers.astype(BF16), vb, NN) / total).astype(BF16)

    for m in range(3):
        for d in range(2):
            run[d, m, 0] = local(m, r_slab(d, m, 0)).astype(BF16)
            r_copy(d, m, 0).start()
        attend(m)

    def reduce_turn(s, carry):
        for m in range(3):
            for d in range(2):
                r_copy(d, m, s - 1).wait_recv()
                run[d, m, s] = (run[d, m, s].astype(F32) + local(m, r_slab(d, m, s))).astype(BF16)
                r_copy(d, m, s).start()
            attend(s * 3 + m)
        return carry

    lax.fori_loop(1, 7, reduce_turn, 0)
    for m in range(3):
        for d in range(2):
            if SENDS[m][d] == 8:
                r_copy(d, m, 6).wait_recv()
                run[d, m, 7] = (run[d, m, 7].astype(F32) + local(m, r_slab(d, m, 7))).astype(BF16)
                r_copy(d, m, 7).start()
        attend(21 + m)

    def q_copy(m):
        return remote(sq_mine.at[m], sq_sib.at[m], q_send.at[m], q_recv.at[m], sib)

    for m in range(3):
        total = local(m, z)
        for d in range(2):
            last = SENDS[m][d]
            r_copy(d, m, last - 1).wait_recv()
            total += run[d, m, last].astype(F32)
        new = w_t[m, :, mine] - total
        fresh[m] = new
        sq_mine[m] = jnp.broadcast_to(jnp.sum(new * new, axis=1, keepdims=True), (SLAB, 128))
        q_copy(m).start()
    for m in range(3):
        old = w_t[m]
        old_ms = jnp.mean(old * old, axis=1, keepdims=True)
        q_copy(m).wait()
        new_ms = (sq_mine[m, :, 0:1] + sq_sib[m, :, 0:1]) * (1.0 / FD)
        u_all[m, rows(z), mine] = (fresh[m] * (jnp.sqrt(old_ms) * lax.rsqrt(new_ms + 1e-06))).astype(BF16)

    def own_copy(m):
        view = u_all.at[m, rows(z), mine]
        return remote(view, view, ud_send.at[0, m, 0], ud_recv.at[0, m, 0], sib)

    for m in range(3):
        own_copy(m).start()

    ring_gather(u_all, u_send, u_recv, ud_send, ud_recv, lambda s: None)

    for m in range(3):
        own_copy(m).wait()

    def apply_block(b, carry):
        cols = pl.ds(pl.multiple_of(b * 256, 256), 256)
        gate = dot(fq[...], u_all[0, cols, :], NT)
        up = dot(fq[...], u_all[1, cols, :], NT)
        hid[:, cols] = (gate * jax.nn.sigmoid(gate) * up).astype(BF16)
        return carry

    lax.fori_loop(0, 3, apply_block, 0)

    def out_block(b, carry):
        cols = pl.ds(pl.multiple_of(b * 256, 256), 256)
        fout[:, cols] = dot(hid[...], u_all[2, cols, :], NT).astype(BF16)
        return carry

    lax.fori_loop(0, 3, out_block, 0)

    for m in range(3):
        g_copy(m).wait_send()
        for d in range(2):
            for s in range(SENDS[m][d]):
                r_copy(d, m, s).wait_send()
    for copy in halo:
        copy.wait_send()


def body(query_rows, key_rows, value_rows, step_sizes, w_gate, w_up, w_down):
    dma = pltpu.SemaphoreType.DMA
    vmem = pltpu.VMEM
    anywhere = pl.BlockSpec(memory_space=pl.ANY)
    inside = pl.BlockSpec(memory_space=pltpu.VMEM)
    return pl.pallas_call(
        kernel,
        out_shape=(jax.ShapeDtypeStruct((TOK, FD), BF16), jax.ShapeDtypeStruct((TOK, FD), BF16)),
        in_specs=[anywhere] * 3 + [inside] * 4,
        out_specs=(inside, inside),
        scratch_shapes=[
            vmem((TOK, FD), BF16),
            vmem((TOK + WINDOW, FD), BF16),
            vmem((TOK + WINDOW, FD), BF16),
            vmem((TOK, FD), BF16),
            vmem((TOK, FD), BF16),
            vmem((TOK, FD), BF16),
            vmem((3, 32, FD), BF16),
            vmem((3, 32, FD), BF16),
            vmem((3, FD, FD), BF16),
            vmem((3, FD, FD), BF16),
            vmem((3, FD, HALF), BF16),
            vmem((2, 3, 9, SLAB, HALF), BF16),
            vmem((3, SLAB, FD), F32),
            vmem((3, SLAB, HALF), F32),
            vmem((3, SLAB, 128), F32),
            vmem((3, SLAB, 128), F32),
            vmem((3, FD, FD), BF16),
            vmem((TOK, FD), BF16),
            dma((3,)), dma((2,)), dma((2,)), dma, dma,
            dma((2, 3, 8)), dma((2, 3, 8)), dma((2, 3, 9)), dma((2, 3, 9)),
            dma((3,)), dma((3,)), dma((2, 3, 8)), dma((2, 3, 8)), dma((3,)), dma((3,)),
            dma((2, 3, 8)), dma((2, 3, 8)), dma((2, 3, 9)), dma((2, 3, 9)),
        ],
        compiler_params=pltpu.CompilerParams(
            collective_id=0, has_side_effects=True, vmem_limit_bytes=56 * 2**20
        ),
        cost_estimate=pl.CostEstimate(flops=7 * 10**9, bytes_accessed=5 * 10**6, transcendentals=4 * 10**6),
        name="attend_and_update",
    )(query_rows, key_rows, value_rows, step_sizes, w_gate, w_up, w_down)


def solution(mesh):
    tokens = P(("seqs", "context"), "fheads")
    weights = P("fheads", "context", None)
    return jax.shard_map(
        body,
        mesh=mesh,
        in_specs=(tokens,) * 4 + (weights,) * 3,
        out_specs=(tokens, tokens),
        check_vma=False,
    )
```

```python
import functools
import math

import jax
import jax.numpy as jnp
from jax import lax
from jax.experimental import pallas as pl
from jax.experimental.pallas import tpu as pltpu
from jax.sharding import PartitionSpec as P

MESH = pl.DeviceIdType.MESH
F32 = jnp.float32
BF16 = jnp.bfloat16
HD = 128
WINDOW = 512
NZ = 16
TOK = 512
FD = 768
SLAB = FD // NZ
UNITS = 9
TOKENS = ((0, 2), (2, 2), (4, 2), (6, 2), (8, 1))
NN = (((1,), (0,)), ((), ()))
NT = (((1,), (1,)), ((), ()))
TN = (((0,), (0,)), ((), ()))


def dot(a, b, dims):
    return lax.dot_general(a, b, dims, preferred_element_type=F32)


def kernel(
    q_in, k_in, v_in, step_ref, wg_ref, wu_ref, wd_ref, wout, fout,
    qs, kcat, vcat, fk, fq, tgt, wpad, wsib, w_all, grad, grad_sib, run, w_t, last_mine, last_sib, u_all,
    hid, d_gate, d_up,
    in_sem, halo_send, halo_recv, pad_send, pad_recv, a_send, a_recv, ad_send, ad_recv,
    g_send, g_recv, r_send, r_recv, f_send, f_recv, u_send, u_recv, ud_send, ud_recv,
):
    c = lax.axis_index("context")
    core = lax.rem(c, 2)
    z = lax.div(c, 2)
    n = 2 * NZ
    sg = 1 - 2 * core
    sib = c + sg
    nxt = lax.rem(c + 2 * sg + n, n)
    following = lax.rem(c + 1, n)
    units = [pl.ds(3 * m, 3) for m in range(3)]
    tokens = [pl.ds(*t) for t in TOKENS]
    all_tokens = range(len(TOKENS))
    is_up = core == 0
    is_down = core == 1

    def around(k):
        return lax.rem(k + 2 * NZ, NZ)

    def remote(src, dst, send, recv, to):
        return pltpu.make_async_remote_copy(
            src_ref=src, dst_ref=dst, send_sem=send, recv_sem=recv, device_id=to, device_id_type=MESH
        )

    to_sib = {"context": sib}
    to_nxt = {"context": nxt}

    loads = (
        pltpu.make_async_copy(k_in, kcat.at[pl.ds(WINDOW, TOK)], in_sem.at[0]),
        pltpu.make_async_copy(v_in, vcat.at[pl.ds(WINDOW, TOK)], in_sem.at[1]),
        pltpu.make_async_copy(q_in, qs, in_sem.at[2]),
    )
    for load in loads:
        load.start()

    barrier = pltpu.get_barrier_semaphore()
    for step in (1, 2, n - 1, n - 2):
        pl.semaphore_signal(
            barrier, inc=1, device_id={"context": lax.rem(c + step, n)}, device_id_type=MESH
        )
    for m, ref in enumerate((wd_ref, wg_ref, wu_ref)):
        block = ref[0].astype(F32)
        wpad[m] = jnp.concatenate([block, jnp.zeros((8, FD), F32)], axis=0).astype(BF16)
    pl.semaphore_wait(barrier, 4)

    pad = remote(wpad, wsib, pad_send, pad_recv, to_sib)
    pad.start()
    pad.wait()
    for m in range(3):
        own = wpad[m].astype(F32)[:24]
        sibs = wsib[m].astype(F32)[:24]
        low = jnp.where(core == 0, own, sibs)
        high = jnp.where(core == 0, sibs, own)
        w_all[z, units[m]] = jnp.concatenate([low, high], axis=0).astype(BF16).reshape(3, 16, FD)

    def away(s):
        return around(z - sg * s)

    def ring(buf, z_send, z_recv, d_send, d_recv):
        def z_copy(t, s):
            view = buf.at[away(s), tokens[t]]
            return remote(view, view, z_send.at[t, s], z_recv.at[t, s], to_nxt)

        def d_copy(s):
            view = buf.at[away(s)]
            return remote(view, view, d_send.at[s], d_recv.at[s], to_sib)

        return z_copy, d_copy

    def pass_on(z_copy, d_copy, filler):
        def turn(s, carry):
            for t in all_tokens:
                z_copy(t, s - 1).wait_recv()
                z_copy(t, s).start()
            d_copy(s).start()
            filler(s)
            return carry

        lax.fori_loop(1, 7, turn, 0)
        for t in all_tokens:
            z_copy(t, 6).wait_recv()
            pl.when(is_up)(lambda: z_copy(t, 7).start())
        d_copy(7).start()

    def collect(z_copy, d_copy):
        @pl.when(is_up)
        def _():
            for t in all_tokens:
                z_copy(t, 7).wait_recv()
            d_copy(8).start()

        for s in range(1, 8):
            d_copy(s).wait_recv()
        pl.when(is_down)(lambda: d_copy(8).wait_recv())

    a_copy, ad_copy = ring(w_all, a_send, a_recv, ad_send, ad_recv)
    u_copy, ud_copy = ring(u_all, u_send, u_recv, ud_send, ud_recv)

    halo = (
        remote(kcat.at[pl.ds(WINDOW, TOK)], kcat.at[pl.ds(0, WINDOW)], halo_send.at[0], halo_recv.at[0], {"context": following}),
        remote(vcat.at[pl.ds(WINDOW, TOK)], vcat.at[pl.ds(0, WINDOW)], halo_send.at[1], halo_recv.at[1], {"context": following}),
    )

    for t in all_tokens:
        a_copy(t, 0).start()
    for load in loads:
        load.wait()

    def prepare(b, carry):
        r = pl.ds(pl.multiple_of(b * 64, 64), 64)
        near = pl.ds(pl.multiple_of(b * 64 + WINDOW, 64), 64)
        k = kcat[near, :].astype(F32)
        fk[r, :] = (k * lax.rsqrt(jnp.mean(k * k, axis=-1, keepdims=True) + 1e-06)).astype(BF16)
        x = qs[r, :].astype(F32)
        fq[r, :] = (x * lax.rsqrt(jnp.mean(x * x, axis=-1, keepdims=True) + 1e-06)).astype(BF16)
        return carry

    lax.fori_loop(0, 8, prepare, 0)
    for b in range(TOK // 128):
        step = jnp.transpose(jnp.broadcast_to(step_ref[b : b + 1, :], (128, 128)))[:, 0:1]
        near = pl.ds(b * 128 + WINDOW, 128)
        tgt[b * 128 : b * 128 + 128, :] = (-(step * vcat[near, :].astype(F32))).astype(BF16)

    pass_on(a_copy, ad_copy, lambda s: None)
    for copy in halo:
        copy.start()
    collect(a_copy, ad_copy)

    def whole(buf, m):
        return buf[:, units[m]].reshape(FD, FD)

    give = pl.ds(jnp.where(core == 0, 8, 1), 8)

    def g_copy(m):
        return remote(grad.at[give, units[m]], grad_sib.at[:, units[m]], g_send.at[m], g_recv.at[m], to_sib)

    def local(t, s):
        away_by = 8 - s
        theirs = jnp.where(core == 0, away_by - 1, 8 - away_by)
        return grad[around(sg * away_by), tokens[t]].astype(F32) + grad_sib[theirs, tokens[t]].astype(F32)

    def r_copy(t, s):
        return remote(run.at[s, tokens[t]], run.at[s + 1, tokens[t]], r_send.at[t, s], r_recv.at[t, s], to_nxt)

    def gradient(m, a, b):
        full = dot(a[...], b[...], TN).astype(BF16).reshape(NZ, 3, 16, FD)
        for k in range(NZ):
            grad[around(k - z), units[m]] = full[k]
        g_copy(m).start()

    def begin(first, last):
        for s, here in ((0, is_up), (1, is_down)):

            @pl.when(here)
            def _():
                for t in range(first, last):
                    run[s, tokens[t]] = local(t, s).astype(BF16)
                    r_copy(t, s).start()

    gate = dot(fk[...], whole(w_all, 1), NN)
    up = dot(fk[...], whole(w_all, 2), NN)
    sg_gate = jax.nn.sigmoid(gate)
    hid[...] = (gate * sg_gate * up).astype(BF16)
    gradient(0, tgt, hid)
    back = dot(tgt[...], whole(w_all, 0), NT)
    d_gate[...] = (back * up * sg_gate * (1.0 + gate * (1.0 - sg_gate))).astype(BF16)
    d_up[...] = (back * gate * sg_gate).astype(BF16)
    g_copy(0).wait_recv()
    begin(0, 1)
    gradient(1, d_gate, fk)
    gradient(2, d_up, fk)
    g_copy(1).wait_recv()
    begin(1, 2)
    g_copy(2).wait_recv()
    begin(2, 5)

    pick = (
        lax.broadcasted_iota(jnp.int32, (SLAB, FD), 1)
        == lax.broadcasted_iota(jnp.int32, (SLAB, FD), 0) + z * SLAB
    ).astype(BF16)
    for m in range(3):
        w_t[m] = dot(pick, whole(w_all, m), NT)

    def reduce_step(t, s):
        r_copy(t, s - 1).wait_recv()
        run[s, tokens[t]] = (run[s, tokens[t]].astype(F32) + local(t, s)).astype(BF16)
        r_copy(t, s).start()

    @pl.when(is_up)
    def _():
        for t in all_tokens:
            reduce_step(t, 1)

    def reduce_turn(s, carry):
        for t in all_tokens:
            reduce_step(t, s)
        return carry

    lax.fori_loop(2, 8, reduce_turn, 0)

    def f_copy(m):
        return remote(last_mine.at[units[m]], last_sib.at[units[m]], f_send.at[m], f_recv.at[m], to_sib)

    for m, ready in enumerate(((0, 1), (2,), (3, 4))):
        for t in ready:
            r_copy(t, 7).wait_recv()
        last_mine[units[m]] = (run[8, units[m]].astype(F32) + grad[0, units[m]].astype(F32)).astype(BF16)
        f_copy(m).start()

    for m, ready in enumerate(((0,), (1, 2), (3, 4))):
        old = w_t[m]
        old_ms = jnp.mean(old * old, axis=1, keepdims=True)
        f_copy(m).wait_recv()
        total = last_mine[units[m]].astype(F32) + last_sib[units[m]].astype(F32)
        new = old - total.reshape(SLAB, FD)
        new_ms = jnp.mean(new * new, axis=1, keepdims=True)
        u_all[z, units[m]] = (new * (jnp.sqrt(old_ms) * lax.rsqrt(new_ms + 1e-06))).astype(BF16).reshape(3, 16, FD)
        for t in ready:
            u_copy(t, 0).start()

    for copy in halo:
        copy.wait_recv()
    low_limit = jnp.where(c == 0, WINDOW, 0)

    def attend(piece):
        h = lax.div(piece, 4)
        first = pl.multiple_of(lax.rem(piece, 4) * 128, 128)
        cols = pl.ds(pl.multiple_of(h * HD, HD), HD)
        kb = kcat[pl.ds(first, 640), cols]
        vb = vcat[pl.ds(first, 640), cols]
        scores = dot(qs[pl.ds(first, 128), cols], kb, NT) * (1.0 / math.sqrt(HD))
        t = lax.broadcasted_iota(jnp.int32, (128, 640), 0)
        j = lax.broadcasted_iota(jnp.int32, (128, 640), 1)
        allowed = (j > t) & (j <= t + WINDOW) & (j + first >= low_limit)
        scores = jnp.where(allowed, scores, -1e30)
        powers = jnp.exp(scores - jnp.max(scores, axis=-1, keepdims=True))
        total = jnp.sum(powers, axis=-1, keepdims=True)
        wout[pl.ds(first, 128), cols] = (dot(powers.astype(BF16), vb, NN) / total).astype(BF16)

    def attend_some(s):
        for k in range(3):
            attend(3 * s + k)

    attend_some(0)
    pass_on(u_copy, ud_copy, attend_some)
    attend_some(7)
    collect(u_copy, ud_copy)

    gate = dot(fq[...], whole(u_all, 1), NT)
    up = dot(fq[...], whole(u_all, 2), NT)
    hid[...] = (gate * jax.nn.sigmoid(gate) * up).astype(BF16)
    fout[...] = dot(hid[...], whole(u_all, 0), NT).astype(BF16)

    def sent(s, carry):
        ad_copy(s + 1).wait_send()
        ud_copy(s + 1).wait_send()
        for t in all_tokens:
            a_copy(t, s).wait_send()
            r_copy(t, s + 1).wait_send()
            u_copy(t, s).wait_send()
        return carry

    lax.fori_loop(0, 7, sent, 0)

    @pl.when(is_up)
    def _():
        ad_copy(8).wait_send()
        ud_copy(8).wait_send()
        for t in all_tokens:
            a_copy(t, 7).wait_send()
            r_copy(t, 0).wait_send()
            u_copy(t, 7).wait_send()

    for m in range(3):
        g_copy(m).wait_send()
        f_copy(m).wait_send()
    for copy in halo:
        copy.wait_send()


def body(query_rows, key_rows, value_rows, step_sizes, w_gate, w_up, w_down):
    dma = pltpu.SemaphoreType.DMA
    vmem = pltpu.VMEM
    anywhere = pl.BlockSpec(memory_space=pl.ANY)
    inside = pl.BlockSpec(memory_space=pltpu.VMEM)
    slabs = (NZ, UNITS, 16, FD)
    return pl.pallas_call(
        kernel,
        out_shape=(jax.ShapeDtypeStruct((TOK, FD), BF16), jax.ShapeDtypeStruct((TOK, FD), BF16)),
        in_specs=[anywhere] * 3 + [inside] * 4,
        out_specs=(inside, inside),
        scratch_shapes=[
            vmem((TOK, FD), BF16),
            vmem((TOK + WINDOW, FD), BF16),
            vmem((TOK + WINDOW, FD), BF16),
            vmem((TOK, FD), BF16),
            vmem((TOK, FD), BF16),
            vmem((TOK, FD), BF16),
            vmem((3, 32, FD), BF16),
            vmem((3, 32, FD), BF16),
            vmem(slabs, BF16),
            vmem(slabs, BF16),
            vmem((8, UNITS, 16, FD), BF16),
            vmem((9, UNITS, 16, FD), BF16),
            vmem((3, SLAB, FD), F32),
            vmem((UNITS, 16, FD), BF16),
            vmem((UNITS, 16, FD), BF16),
            vmem(slabs, BF16),
            vmem((TOK, FD), BF16),
            vmem((TOK, FD), BF16),
            vmem((TOK, FD), BF16),
            dma((3,)), dma((2,)), dma((2,)), dma, dma,
            dma((5, 8)), dma((5, 8)), dma((9,)), dma((9,)),
            dma((3,)), dma((3,)), dma((5, 8)), dma((5, 8)), dma((3,)), dma((3,)),
            dma((5, 8)), dma((5, 8)), dma((9,)), dma((9,)),
        ],
        compiler_params=pltpu.CompilerParams(
            collective_id=0, has_side_effects=True, vmem_limit_bytes=56 * 2**20
        ),
        cost_estimate=pl.CostEstimate(flops=7 * 10**9, bytes_accessed=5 * 10**6, transcendentals=4 * 10**6),
        name="attend_and_update",
    )(query_rows, key_rows, value_rows, step_sizes.reshape(TOK // 128, 128), w_gate, w_up, w_down)


def solution(mesh):
    tokens = P(("seqs", "context"), "fheads")
    weights = P("fheads", "context", None)
    return jax.shard_map(
        body,
        mesh=mesh,
        in_specs=(tokens,) * 4 + (weights,) * 3,
        out_specs=(tokens, tokens),
        check_vma=False,
    )
```

```python
import functools
import math

import jax
import jax.numpy as jnp
from jax import lax
from jax.experimental import pallas as pl
from jax.experimental.pallas import tpu as pltpu
from jax.sharding import PartitionSpec as P

MESH = pl.DeviceIdType.MESH
F32 = jnp.float32
BF16 = jnp.bfloat16
HD = 128
WINDOW = 512
NZ = 16
TOK = 512
FD = 768
SLAB = FD // NZ
UNITS = 9
TOKENS = ((0, 2), (2, 2), (4, 2), (6, 2), (8, 1))
FIRST_OF = {0: 0, 1: 1, 3: 2}
NN = (((1,), (0,)), ((), ()))
NT = (((1,), (1,)), ((), ()))
TN = (((0,), (0,)), ((), ()))


def dot(a, b, dims):
    return lax.dot_general(a, b, dims, preferred_element_type=F32)


def kernel(
    q_in, k_in, v_in, step_ref, wg_ref, wu_ref, wd_ref, out,
    qs, kcat, vcat, fk, fq, tgt, wpad, wsib, w_all, grad, grad_sib, run, w_t, last_mine, last_sib, u_all,
    hid, d_gate, d_up,
    in_sem, halo_send, halo_recv, pad_send, pad_recv, a_send, a_recv, ad_send, ad_recv,
    g_send, g_recv, r_send, r_recv, f_send, f_recv, u_send, u_recv, ud_send, ud_recv,
):
    c = lax.axis_index("context")
    core = lax.rem(c, 2)
    z = lax.div(c, 2)
    n = 2 * NZ
    sg = 2 * core - 1
    sib = c - sg
    nxt = lax.rem(c + 2 * sg + n, n)
    following = lax.rem(c + 1, n)
    units = [pl.ds(3 * m, 3) for m in range(3)]
    tokens = [pl.ds(*t) for t in TOKENS]
    all_tokens = range(len(TOKENS))
    is_far = core == 0
    is_near = core == 1

    def around(k):
        return lax.rem(k + 2 * NZ, NZ)

    def remote(src, dst, send, recv, to):
        return pltpu.make_async_remote_copy(
            src_ref=src, dst_ref=dst, send_sem=send, recv_sem=recv, device_id=to, device_id_type=MESH
        )

    to_sib = {"context": sib}
    to_nxt = {"context": nxt}

    loads = (
        pltpu.make_async_copy(k_in, kcat.at[pl.ds(WINDOW, TOK)], in_sem.at[0]),
        pltpu.make_async_copy(v_in, vcat.at[pl.ds(WINDOW, TOK)], in_sem.at[1]),
        pltpu.make_async_copy(q_in, qs, in_sem.at[2]),
    )
    for load in loads:
        load.start()

    barrier = pltpu.get_barrier_semaphore()
    for step in (1, 2, n - 1, n - 2):
        pl.semaphore_signal(
            barrier, inc=1, device_id={"context": lax.rem(c + step, n)}, device_id_type=MESH
        )
    for m, ref in enumerate((wd_ref, wg_ref, wu_ref)):
        block = ref[0].astype(F32)
        wpad[m] = jnp.concatenate([block, jnp.zeros((8, FD), F32)], axis=0).astype(BF16)
    pl.semaphore_wait(barrier, 4)

    pad = remote(wpad, wsib, pad_send, pad_recv, to_sib)
    pad.start()
    pad.wait()
    for m in range(3):
        own = wpad[m].astype(F32)[:24]
        sibs = wsib[m].astype(F32)[:24]
        low = jnp.where(core == 0, own, sibs)
        high = jnp.where(core == 0, sibs, own)
        w_all[z, units[m]] = jnp.concatenate([low, high], axis=0).astype(BF16).reshape(3, 16, FD)

    def away(s):
        return around(z - sg * s)

    def ring(buf, z_send, z_recv, d_send, d_recv):
        def z_copy(t, s):
            view = buf.at[away(s), tokens[t]]
            return remote(view, view, z_send.at[t, s], z_recv.at[t, s], to_nxt)

        def d_copy(s):
            view = buf.at[away(s)]
            return remote(view, view, d_send.at[s], d_recv.at[s], to_sib)

        return z_copy, d_copy

    def pass_on(z_copy, d_copy, filler):
        def turn(s, carry):
            for t in all_tokens:
                z_copy(t, s - 1).wait_recv()
                z_copy(t, s).start()
            d_copy(s).start()
            filler(s)
            return carry

        lax.fori_loop(1, 7, turn, 0)
        for t in all_tokens:
            z_copy(t, 6).wait_recv()
            pl.when(is_far)(lambda: z_copy(t, 7).start())
        d_copy(7).start()

    def collect(z_copy, d_copy):
        @pl.when(is_far)
        def _():
            for t in all_tokens:
                z_copy(t, 7).wait_recv()
            d_copy(8).start()

        for s in range(1, 8):
            d_copy(s).wait_recv()
        pl.when(is_near)(lambda: d_copy(8).wait_recv())

    a_copy, ad_copy = ring(w_all, a_send, a_recv, ad_send, ad_recv)
    u_copy, ud_copy = ring(u_all, u_send, u_recv, ud_send, ud_recv)

    halo = (
        remote(kcat.at[pl.ds(WINDOW, TOK)], kcat.at[pl.ds(0, WINDOW)], halo_send.at[0], halo_recv.at[0], {"context": following}),
        remote(vcat.at[pl.ds(WINDOW, TOK)], vcat.at[pl.ds(0, WINDOW)], halo_send.at[1], halo_recv.at[1], {"context": following}),
    )

    for t in all_tokens:
        a_copy(t, 0).start()
    for load in loads:
        load.wait()

    def prepare(b, carry):
        r = pl.ds(pl.multiple_of(b * 64, 64), 64)
        near = pl.ds(pl.multiple_of(b * 64 + WINDOW, 64), 64)
        k = kcat[near, :].astype(F32)
        fk[r, :] = (k * lax.rsqrt(jnp.mean(k * k, axis=-1, keepdims=True) + 1e-06)).astype(BF16)
        x = qs[r, :].astype(F32)
        fq[r, :] = (x * lax.rsqrt(jnp.mean(x * x, axis=-1, keepdims=True) + 1e-06)).astype(BF16)
        return carry

    lax.fori_loop(0, 8, prepare, 0)
    for b in range(TOK // 128):
        step = jnp.transpose(jnp.broadcast_to(step_ref[b : b + 1, :], (128, 128)))[:, 0:1]
        near = pl.ds(b * 128 + WINDOW, 128)
        tgt[b * 128 : b * 128 + 128, :] = (-(step * vcat[near, :].astype(F32))).astype(BF16)

    pass_on(a_copy, ad_copy, lambda s: None)
    for copy in halo:
        copy.start()
    collect(a_copy, ad_copy)

    def whole(buf, m):
        return buf[:, units[m]].reshape(FD, FD)

    def g_copy(m, s):
        return remote(
            grad.at[around(sg * (s - 8)), units[m]], grad_sib.at[s, units[m]],
            g_send.at[m, s], g_recv.at[m, s], to_sib,
        )

    def local(t, s):
        return grad[around(sg * (8 - s)), tokens[t]].astype(F32) + grad_sib[s, tokens[t]].astype(F32)

    def r_copy(t, s):
        return remote(run.at[s, tokens[t]], run.at[s + 1, tokens[t]], r_send.at[t, s], r_recv.at[t, s], to_nxt)

    def gradient(m, a, b):
        full = dot(a[...], b[...], TN).astype(BF16).reshape(NZ, 3, 16, FD)
        for k in range(NZ):
            grad[around(k - z), units[m]] = full[k]
        pl.when(is_near)(lambda: g_copy(m, 0).start())
        for s in range(1, 8):
            g_copy(m, s).start()

    def begin(first, last):
        for s, here in ((0, is_far), (1, is_near)):

            @pl.when(here)
            def _():
                for t in range(first, last):
                    if t in FIRST_OF:
                        g_copy(FIRST_OF[t], s).wait_recv()
                    run[s, tokens[t]] = local(t, s).astype(BF16)
                    r_copy(t, s).start()

    gate = dot(fk[...], whole(w_all, 1), NN)
    up = dot(fk[...], whole(w_all, 2), NN)
    sg_gate = jax.nn.sigmoid(gate)
    hid[...] = (gate * sg_gate * up).astype(BF16)
    gradient(0, tgt, hid)
    back = dot(tgt[...], whole(w_all, 0), NT)
    d_gate[...] = (back * up * sg_gate * (1.0 + gate * (1.0 - sg_gate))).astype(BF16)
    d_up[...] = (back * gate * sg_gate).astype(BF16)
    begin(0, 1)
    gradient(1, d_gate, fk)
    gradient(2, d_up, fk)
    begin(1, 5)

    pick = (
        lax.broadcasted_iota(jnp.int32, (SLAB, FD), 1)
        == lax.broadcasted_iota(jnp.int32, (SLAB, FD), 0) + z * SLAB
    ).astype(BF16)
    for m in range(3):
        w_t[m] = dot(pick, whole(w_all, m), NT)

    def reduce_step(t, s):
        r_copy(t, s - 1).wait_recv()
        if t in FIRST_OF:
            g_copy(FIRST_OF[t], s).wait_recv()
        run[s, tokens[t]] = (run[s, tokens[t]].astype(F32) + local(t, s)).astype(BF16)
        r_copy(t, s).start()

    @pl.when(is_far)
    def _():
        for t in all_tokens:
            reduce_step(t, 1)

    def reduce_turn(s, carry):
        for t in all_tokens:
            reduce_step(t, s)
        return carry

    lax.fori_loop(2, 8, reduce_turn, 0)

    def f_copy(m):
        return remote(last_mine.at[units[m]], last_sib.at[units[m]], f_send.at[m], f_recv.at[m], to_sib)

    for m, ready in enumerate(((0, 1), (2,), (3, 4))):
        for t in ready:
            r_copy(t, 7).wait_recv()
        last_mine[units[m]] = (run[8, units[m]].astype(F32) + grad[0, units[m]].astype(F32)).astype(BF16)
        f_copy(m).start()

    for m, ready in enumerate(((0,), (1, 2), (3, 4))):
        old = w_t[m]
        old_ms = jnp.mean(old * old, axis=1, keepdims=True)
        f_copy(m).wait_recv()
        total = last_mine[units[m]].astype(F32) + last_sib[units[m]].astype(F32)
        new = old - total.reshape(SLAB, FD)
        new_ms = jnp.mean(new * new, axis=1, keepdims=True)
        u_all[z, units[m]] = (new * (jnp.sqrt(old_ms) * lax.rsqrt(new_ms + 1e-06))).astype(BF16).reshape(3, 16, FD)
        for t in ready:
            u_copy(t, 0).start()

    for copy in halo:
        copy.wait_recv()
    low_limit = jnp.where(c == 0, WINDOW, 0)

    def attend(piece):
        h = lax.div(piece, 4)
        first = pl.multiple_of(lax.rem(piece, 4) * 128, 128)
        cols = pl.ds(pl.multiple_of(h * HD, HD), HD)
        kb = kcat[pl.ds(first, 640), cols]
        vb = vcat[pl.ds(first, 640), cols]
        scores = dot(qs[pl.ds(first, 128), cols], kb, NT) * (1.0 / math.sqrt(HD))
        t = lax.broadcasted_iota(jnp.int32, (128, 640), 0)
        j = lax.broadcasted_iota(jnp.int32, (128, 640), 1)
        allowed = (j > t) & (j <= t + WINDOW) & (j + first >= low_limit)
        scores = jnp.where(allowed, scores, -1e30)
        powers = jnp.exp(scores - jnp.max(scores, axis=-1, keepdims=True))
        total = jnp.sum(powers, axis=-1, keepdims=True)
        out[0, pl.ds(first, 128), cols] = (dot(powers.astype(BF16), vb, NN) / total).astype(BF16)

    def attend_some(s):
        for k in range(3):
            attend(3 * s + k)

    attend_some(0)
    pass_on(u_copy, ud_copy, attend_some)
    attend_some(7)
    collect(u_copy, ud_copy)

    gate = dot(fq[...], whole(u_all, 1), NT)
    up = dot(fq[...], whole(u_all, 2), NT)
    hid[...] = (gate * jax.nn.sigmoid(gate) * up).astype(BF16)
    out[1] = dot(hid[...], whole(u_all, 0), NT).astype(BF16)

    def sent(s, carry):
        ad_copy(s + 1).wait_send()
        ud_copy(s + 1).wait_send()
        for t in all_tokens:
            a_copy(t, s).wait_send()
            r_copy(t, s + 1).wait_send()
            u_copy(t, s).wait_send()
        return carry

    lax.fori_loop(0, 7, sent, 0)

    @pl.when(is_far)
    def _():
        ad_copy(8).wait_send()
        ud_copy(8).wait_send()
        for t in all_tokens:
            a_copy(t, 7).wait_send()
            r_copy(t, 0).wait_send()
            u_copy(t, 7).wait_send()

    for m in range(3):
        pl.when(is_near)(lambda: g_copy(m, 0).wait_send())
        for s in range(1, 8):
            g_copy(m, s).wait_send()
        f_copy(m).wait_send()
    for copy in halo:
        copy.wait_send()


def body(query_rows, key_rows, value_rows, step_sizes, w_gate, w_up, w_down):
    dma = pltpu.SemaphoreType.DMA
    vmem = pltpu.VMEM
    anywhere = pl.BlockSpec(memory_space=pl.ANY)
    inside = pl.BlockSpec(memory_space=pltpu.VMEM)
    slabs = (NZ, UNITS, 16, FD)
    out = pl.pallas_call(
        kernel,
        out_shape=jax.ShapeDtypeStruct((2, TOK, FD), BF16),
        in_specs=[anywhere] * 3 + [inside] * 4,
        out_specs=inside,
        scratch_shapes=[
            vmem((TOK, FD), BF16),
            vmem((TOK + WINDOW, FD), BF16),
            vmem((TOK + WINDOW, FD), BF16),
            vmem((TOK, FD), BF16),
            vmem((TOK, FD), BF16),
            vmem((TOK, FD), BF16),
            vmem((3, 32, FD), BF16),
            vmem((3, 32, FD), BF16),
            vmem(slabs, BF16),
            vmem(slabs, BF16),
            vmem((8, UNITS, 16, FD), BF16),
            vmem((9, UNITS, 16, FD), BF16),
            vmem((3, SLAB, FD), F32),
            vmem((UNITS, 16, FD), BF16),
            vmem((UNITS, 16, FD), BF16),
            vmem(slabs, BF16),
            vmem((TOK, FD), BF16),
            vmem((TOK, FD), BF16),
            vmem((TOK, FD), BF16),
            dma((3,)), dma((2,)), dma((2,)), dma, dma,
            dma((5, 8)), dma((5, 8)), dma((9,)), dma((9,)),
            dma((3, 8)), dma((3, 8)), dma((5, 8)), dma((5, 8)), dma((3,)), dma((3,)),
            dma((5, 8)), dma((5, 8)), dma((9,)), dma((9,)),
        ],
        compiler_params=pltpu.CompilerParams(
            collective_id=0, has_side_effects=True, vmem_limit_bytes=56 * 2**20
        ),
        cost_estimate=pl.CostEstimate(flops=7 * 10**9, bytes_accessed=5 * 10**6, transcendentals=4 * 10**6),
        name="attend_and_update",
    )(query_rows, key_rows, value_rows, step_sizes.reshape(TOK // 128, 128), w_gate, w_up, w_down)
    return out[0], out[1]


def solution(mesh):
    tokens = P(("seqs", "context"), "fheads")
    weights = P("fheads", "context", None)
    return jax.shard_map(
        body,
        mesh=mesh,
        in_specs=(tokens,) * 4 + (weights,) * 3,
        out_specs=(tokens, tokens),
        check_vma=False,
    )
```

```python
import functools
import math

import jax
import jax.numpy as jnp
from jax import lax
from jax.experimental import pallas as pl
from jax.experimental.pallas import tpu as pltpu
from jax.sharding import PartitionSpec as P

MESH = pl.DeviceIdType.MESH
F32 = jnp.float32
BF16 = jnp.bfloat16
HD = 128
WINDOW = 512
NZ = 16
TOK = 512
FD = 768
SLAB = FD // NZ
UNITS = 9
TOKENS = ((0, 2), (2, 2), (4, 2), (6, 2), (8, 1))
FIRST_OF = {0: 0, 1: 1, 3: 2}
NN = (((1,), (0,)), ((), ()))
NT = (((1,), (1,)), ((), ()))
TN = (((0,), (0,)), ((), ()))


def dot(a, b, dims):
    return lax.dot_general(a, b, dims, preferred_element_type=F32)


def kernel(
    q_in, k_in, v_in, step_ref, wg_ref, wu_ref, wd_ref, out,
    qs, kcat, vcat, fk, fq, tgt, wpad, wsib, w_all, grad, grad_sib, run, w_t, last_mine, last_sib, u_all,
    hid, d_gate, d_up,
    in_sem, halo_send, halo_recv, pad_send, pad_recv, a_send, a_recv, ad_send, ad_recv,
    g_send, g_recv, r_send, r_recv, f_send, f_recv, u_send, u_recv, ud_send, ud_recv,
):
    c = lax.axis_index("context")
    core = lax.rem(c, 2)
    z = lax.div(c, 2)
    n = 2 * NZ
    sg = 2 * core - 1
    sib = c - sg
    nxt = lax.rem(c + 2 * sg + n, n)
    following = lax.rem(c + 1, n)
    units = [pl.ds(3 * m, 3) for m in range(3)]
    tokens = [pl.ds(*t) for t in TOKENS]
    all_tokens = range(len(TOKENS))
    is_far = core == 0
    is_near = core == 1

    def around(k):
        return lax.rem(k + 2 * NZ, NZ)

    def remote(src, dst, send, recv, to):
        return pltpu.make_async_remote_copy(
            src_ref=src, dst_ref=dst, send_sem=send, recv_sem=recv, device_id=to, device_id_type=MESH
        )

    to_sib = {"context": sib}
    to_nxt = {"context": nxt}

    loads = (
        pltpu.make_async_copy(k_in, kcat.at[pl.ds(WINDOW, TOK)], in_sem.at[0]),
        pltpu.make_async_copy(v_in, vcat.at[pl.ds(WINDOW, TOK)], in_sem.at[1]),
        pltpu.make_async_copy(q_in, qs, in_sem.at[2]),
    )
    for load in loads:
        load.start()

    barrier = pltpu.get_barrier_semaphore()
    for step in (1, 2, n - 1, n - 2):
        pl.semaphore_signal(
            barrier, inc=1, device_id={"context": lax.rem(c + step, n)}, device_id_type=MESH
        )
    for m, ref in enumerate((wd_ref, wg_ref, wu_ref)):
        block = ref[0].astype(F32)
        wpad[m] = jnp.concatenate([block, jnp.zeros((8, FD), F32)], axis=0).astype(BF16)
    pl.semaphore_wait(barrier, 4)

    pad = remote(wpad, wsib, pad_send, pad_recv, to_sib)
    pad.start()
    pad.wait()
    for m in range(3):
        own = wpad[m].astype(F32)[:24]
        sibs = wsib[m].astype(F32)[:24]
        low = jnp.where(core == 0, own, sibs)
        high = jnp.where(core == 0, sibs, own)
        w_all[z, units[m]] = jnp.concatenate([low, high], axis=0).astype(BF16).reshape(3, 16, FD)

    def away(s):
        return around(z - sg * s)

    def ring(buf, z_send, z_recv, d_send, d_recv):
        def z_copy(t, s):
            view = buf.at[away(s), tokens[t]]
            return remote(view, view, z_send.at[t, s], z_recv.at[t, s], to_nxt)

        def d_copy(s):
            view = buf.at[away(s)]
            return remote(view, view, d_send.at[s], d_recv.at[s], to_sib)

        return z_copy, d_copy

    def pass_on(z_copy, d_copy, filler):
        def turn(s, carry):
            for t in all_tokens:
                z_copy(t, s - 1).wait_recv()
                z_copy(t, s).start()
            d_copy(s).start()
            filler(s)
            return carry

        lax.fori_loop(1, 7, turn, 0)
        for t in all_tokens:
            z_copy(t, 6).wait_recv()
            pl.when(is_far)(lambda: z_copy(t, 7).start())
        d_copy(7).start()

    def collect(z_copy, d_copy):
        @pl.when(is_far)
        def _():
            for t in all_tokens:
                z_copy(t, 7).wait_recv()
            d_copy(8).start()

        for s in range(1, 8):
            d_copy(s).wait_recv()
        pl.when(is_near)(lambda: d_copy(8).wait_recv())

    a_copy, ad_copy = ring(w_all, a_send, a_recv, ad_send, ad_recv)
    u_copy, ud_copy = ring(u_all, u_send, u_recv, ud_send, ud_recv)

    halo = (
        remote(kcat.at[pl.ds(WINDOW, TOK)], kcat.at[pl.ds(0, WINDOW)], halo_send.at[0], halo_recv.at[0], {"context": following}),
        remote(vcat.at[pl.ds(WINDOW, TOK)], vcat.at[pl.ds(0, WINDOW)], halo_send.at[1], halo_recv.at[1], {"context": following}),
    )

    for t in all_tokens:
        a_copy(t, 0).start()
    for load in loads:
        load.wait()

    def prepare(b, carry):
        r = pl.ds(pl.multiple_of(b * 64, 64), 64)
        near = pl.ds(pl.multiple_of(b * 64 + WINDOW, 64), 64)
        k = kcat[near, :].astype(F32)
        fk[r, :] = (k * lax.rsqrt(jnp.mean(k * k, axis=-1, keepdims=True) + 1e-06)).astype(BF16)
        x = qs[r, :].astype(F32)
        fq[r, :] = (x * lax.rsqrt(jnp.mean(x * x, axis=-1, keepdims=True) + 1e-06)).astype(BF16)
        return carry

    lax.fori_loop(0, 8, prepare, 0)
    for b in range(TOK // 128):
        step = jnp.transpose(jnp.broadcast_to(step_ref[b : b + 1, :], (128, 128)))[:, 0:1]
        near = pl.ds(b * 128 + WINDOW, 128)
        tgt[b * 128 : b * 128 + 128, :] = (-(step * vcat[near, :].astype(F32))).astype(BF16)

    pass_on(a_copy, ad_copy, lambda s: pl.when(s == 5)(halo[0].start))
    halo[1].start()
    collect(a_copy, ad_copy)

    def whole(buf, m):
        return buf[:, units[m]].reshape(FD, FD)

    def g_copy(m, s):
        return remote(
            grad.at[around(sg * (s - 8)), units[m]], grad_sib.at[s, units[m]],
            g_send.at[m, s], g_recv.at[m, s], to_sib,
        )

    def local(t, s):
        return grad[around(sg * (8 - s)), tokens[t]].astype(F32) + grad_sib[s, tokens[t]].astype(F32)

    def r_copy(t, s):
        return remote(run.at[s, tokens[t]], run.at[s + 1, tokens[t]], r_send.at[t, s], r_recv.at[t, s], to_nxt)

    def gradient(m, a, b):
        full = dot(a[...], b[...], TN).astype(BF16).reshape(NZ, 3, 16, FD)
        for k in range(NZ):
            grad[around(k - z), units[m]] = full[k]
        pl.when(is_near)(lambda: g_copy(m, 0).start())
        for s in range(1, 8):
            g_copy(m, s).start()

    def begin(first, last):
        for s, here in ((0, is_far), (1, is_near)):

            @pl.when(here)
            def _():
                for t in range(first, last):
                    if t in FIRST_OF:
                        g_copy(FIRST_OF[t], s).wait_recv()
                    run[s, tokens[t]] = local(t, s).astype(BF16)
                    r_copy(t, s).start()

    gate = dot(fk[...], whole(w_all, 1), NN)
    up = dot(fk[...], whole(w_all, 2), NN)
    sg_gate = jax.nn.sigmoid(gate)
    hid[...] = (gate * sg_gate * up).astype(BF16)
    gradient(0, tgt, hid)
    back = dot(tgt[...], whole(w_all, 0), NT)
    d_gate[...] = (back * up * sg_gate * (1.0 + gate * (1.0 - sg_gate))).astype(BF16)
    d_up[...] = (back * gate * sg_gate).astype(BF16)
    begin(0, 1)
    gradient(1, d_gate, fk)
    gradient(2, d_up, fk)
    begin(1, 5)

    pick = (
        lax.broadcasted_iota(jnp.int32, (SLAB, FD), 1)
        == lax.broadcasted_iota(jnp.int32, (SLAB, FD), 0) + z * SLAB
    ).astype(BF16)
    for m in range(3):
        w_t[m] = dot(pick, whole(w_all, m), NT)

    def reduce_step(t, s):
        r_copy(t, s - 1).wait_recv()
        if t in FIRST_OF:
            g_copy(FIRST_OF[t], s).wait_recv()
        run[s, tokens[t]] = (run[s, tokens[t]].astype(F32) + local(t, s)).astype(BF16)
        r_copy(t, s).start()

    @pl.when(is_far)
    def _():
        for t in all_tokens:
            reduce_step(t, 1)

    def reduce_turn(s, carry):
        for t in all_tokens:
            reduce_step(t, s)
        return carry

    lax.fori_loop(2, 8, reduce_turn, 0)

    def f_copy(m):
        return remote(last_mine.at[units[m]], last_sib.at[units[m]], f_send.at[m], f_recv.at[m], to_sib)

    for m, ready in enumerate(((0, 1), (2,), (3, 4))):
        for t in ready:
            r_copy(t, 7).wait_recv()
        last_mine[units[m]] = (run[8, units[m]].astype(F32) + grad[0, units[m]].astype(F32)).astype(BF16)
        f_copy(m).start()

    for m, ready in enumerate(((0,), (1, 2), (3, 4))):
        old = w_t[m]
        old_ms = jnp.mean(old * old, axis=1, keepdims=True)
        f_copy(m).wait_recv()
        total = last_mine[units[m]].astype(F32) + last_sib[units[m]].astype(F32)
        new = old - total.reshape(SLAB, FD)
        new_ms = jnp.mean(new * new, axis=1, keepdims=True)
        u_all[z, units[m]] = (new * (jnp.sqrt(old_ms) * lax.rsqrt(new_ms + 1e-06))).astype(BF16).reshape(3, 16, FD)
        for t in ready:
            u_copy(t, 0).start()

    for copy in halo:
        copy.wait_recv()
    low_limit = jnp.where(c == 0, WINDOW, 0)

    def attend(piece):
        h = lax.div(piece, 4)
        first = pl.multiple_of(lax.rem(piece, 4) * 128, 128)
        cols = pl.ds(pl.multiple_of(h * HD, HD), HD)
        kb = kcat[pl.ds(first, 640), cols]
        vb = vcat[pl.ds(first, 640), cols]
        scores = dot(qs[pl.ds(first, 128), cols], kb, NT) * (1.0 / math.sqrt(HD))
        t = lax.broadcasted_iota(jnp.int32, (128, 640), 0)
        j = lax.broadcasted_iota(jnp.int32, (128, 640), 1)
        allowed = (j > t) & (j <= t + WINDOW) & (j + first >= low_limit)
        scores = jnp.where(allowed, scores, -1e30)
        powers = jnp.exp(scores - jnp.max(scores, axis=-1, keepdims=True))
        total = jnp.sum(powers, axis=-1, keepdims=True)
        out[0, pl.ds(first, 128), cols] = (dot(powers.astype(BF16), vb, NN) / total).astype(BF16)

    def attend_some(s):
        for k in range(3):
            attend(3 * s + k)

    attend_some(0)
    pass_on(u_copy, ud_copy, attend_some)
    attend_some(7)
    collect(u_copy, ud_copy)

    gate = dot(fq[...], whole(u_all, 1), NT)
    up = dot(fq[...], whole(u_all, 2), NT)
    hid[...] = (gate * jax.nn.sigmoid(gate) * up).astype(BF16)
    out[1] = dot(hid[...], whole(u_all, 0), NT).astype(BF16)

    def sent(s, carry):
        ad_copy(s + 1).wait_send()
        ud_copy(s + 1).wait_send()
        for t in all_tokens:
            a_copy(t, s).wait_send()
            r_copy(t, s + 1).wait_send()
            u_copy(t, s).wait_send()
        return carry

    lax.fori_loop(0, 7, sent, 0)

    @pl.when(is_far)
    def _():
        ad_copy(8).wait_send()
        ud_copy(8).wait_send()
        for t in all_tokens:
            a_copy(t, 7).wait_send()
            r_copy(t, 0).wait_send()
            u_copy(t, 7).wait_send()

    for m in range(3):
        pl.when(is_near)(lambda: g_copy(m, 0).wait_send())
        for s in range(1, 8):
            g_copy(m, s).wait_send()
        f_copy(m).wait_send()
    for copy in halo:
        copy.wait_send()


def body(query_rows, key_rows, value_rows, step_sizes, w_gate, w_up, w_down):
    dma = pltpu.SemaphoreType.DMA
    vmem = pltpu.VMEM
    anywhere = pl.BlockSpec(memory_space=pl.ANY)
    inside = pl.BlockSpec(memory_space=pltpu.VMEM)
    slabs = (NZ, UNITS, 16, FD)
    out = pl.pallas_call(
        kernel,
        out_shape=jax.ShapeDtypeStruct((2, TOK, FD), BF16),
        in_specs=[anywhere] * 3 + [inside] * 4,
        out_specs=inside,
        scratch_shapes=[
            vmem((TOK, FD), BF16),
            vmem((TOK + WINDOW, FD), BF16),
            vmem((TOK + WINDOW, FD), BF16),
            vmem((TOK, FD), BF16),
            vmem((TOK, FD), BF16),
            vmem((TOK, FD), BF16),
            vmem((3, 32, FD), BF16),
            vmem((3, 32, FD), BF16),
            vmem(slabs, BF16),
            vmem(slabs, BF16),
            vmem((8, UNITS, 16, FD), BF16),
            vmem((9, UNITS, 16, FD), BF16),
            vmem((3, SLAB, FD), F32),
            vmem((UNITS, 16, FD), BF16),
            vmem((UNITS, 16, FD), BF16),
            vmem(slabs, BF16),
            vmem((TOK, FD), BF16),
            vmem((TOK, FD), BF16),
            vmem((TOK, FD), BF16),
            dma((3,)), dma((2,)), dma((2,)), dma, dma,
            dma((5, 8)), dma((5, 8)), dma((9,)), dma((9,)),
            dma((3, 8)), dma((3, 8)), dma((5, 8)), dma((5, 8)), dma((3,)), dma((3,)),
            dma((5, 8)), dma((5, 8)), dma((9,)), dma((9,)),
        ],
        compiler_params=pltpu.CompilerParams(
            collective_id=0, has_side_effects=True, vmem_limit_bytes=56 * 2**20
        ),
        cost_estimate=pl.CostEstimate(flops=7 * 10**9, bytes_accessed=5 * 10**6, transcendentals=4 * 10**6),
        name="attend_and_update",
    )(query_rows, key_rows, value_rows, step_sizes.reshape(TOK // 128, 128), w_gate, w_up, w_down)
    return out[0], out[1]


def solution(mesh):
    tokens = P(("seqs", "context"), "fheads")
    weights = P("fheads", "context", None)
    return jax.shard_map(
        body,
        mesh=mesh,
        in_specs=(tokens,) * 4 + (weights,) * 3,
        out_specs=(tokens, tokens),
        check_vma=False,
    )
```

```python
import functools
import math

import jax
import jax.numpy as jnp
from jax import lax
from jax.experimental import pallas as pl
from jax.experimental.pallas import tpu as pltpu
from jax.sharding import PartitionSpec as P

MESH = pl.DeviceIdType.MESH
F32 = jnp.float32
BF16 = jnp.bfloat16
HD = 128
WINDOW = 512
NZ = 16
TOK = 512
FD = 768
SLAB = FD // NZ
UNITS = 9
TOKENS = ((0, 2), (2, 2), (4, 2), (6, 2), (8, 1))
FIRST_OF = {0: 0, 1: 1, 3: 2}
NN = (((1,), (0,)), ((), ()))
NT = (((1,), (1,)), ((), ()))
TN = (((0,), (0,)), ((), ()))


def dot(a, b, dims):
    return lax.dot_general(a, b, dims, preferred_element_type=F32)


def kernel(
    q_in, k_in, v_in, step_ref, wg_ref, wu_ref, wd_ref, out,
    qs, kcat, vcat, fk, fq, tgt, wpad, wsib, w_all, grad, grad_sib, run, w_t, last_mine, last_sib, u_all,
    hid, d_gate, d_up,
    in_sem, halo_send, halo_recv, pad_send, pad_recv, a_send, a_recv, ad_send, ad_recv,
    g_send, g_recv, r_send, r_recv, f_send, f_recv, u_send, u_recv, ud_send, ud_recv,
):
    c = lax.axis_index("context")
    core = lax.rem(c, 2)
    z = lax.div(c, 2)
    n = 2 * NZ
    sg = 2 * core - 1
    sib = c - sg
    nxt = lax.rem(c + 2 * sg + n, n)
    following = lax.rem(c + 1, n)
    units = [pl.ds(3 * m, 3) for m in range(3)]
    tokens = [pl.ds(*t) for t in TOKENS]
    all_tokens = range(len(TOKENS))
    is_far = core == 0
    is_near = core == 1

    def around(k):
        return lax.rem(k + 2 * NZ, NZ)

    def remote(src, dst, send, recv, to):
        return pltpu.make_async_remote_copy(
            src_ref=src, dst_ref=dst, send_sem=send, recv_sem=recv, device_id=to, device_id_type=MESH
        )

    to_sib = {"context": sib}
    to_nxt = {"context": nxt}

    loads = (
        pltpu.make_async_copy(k_in, kcat.at[pl.ds(WINDOW, TOK)], in_sem.at[0]),
        pltpu.make_async_copy(v_in, vcat.at[pl.ds(WINDOW, TOK)], in_sem.at[1]),
        pltpu.make_async_copy(q_in, qs, in_sem.at[2]),
    )
    for load in loads:
        load.start()

    barrier = pltpu.get_barrier_semaphore()
    for step in (1, 2, n - 1, n - 2):
        pl.semaphore_signal(
            barrier, inc=1, device_id={"context": lax.rem(c + step, n)}, device_id_type=MESH
        )
    for m, ref in enumerate((wd_ref, wg_ref, wu_ref)):
        block = ref[0].astype(F32)
        wpad[m] = jnp.concatenate([block, jnp.zeros((8, FD), F32)], axis=0).astype(BF16)
    pl.semaphore_wait(barrier, 4)

    pad = remote(wpad, wsib, pad_send, pad_recv, to_sib)
    pad.start()
    pad.wait()
    for m in range(3):
        own = wpad[m].astype(F32)[:24]
        sibs = wsib[m].astype(F32)[:24]
        low = jnp.where(core == 0, own, sibs)
        high = jnp.where(core == 0, sibs, own)
        w_all[z, units[m]] = jnp.concatenate([low, high], axis=0).astype(BF16).reshape(3, 16, FD)

    def away(s):
        return around(z - sg * s)

    def ring(buf, z_send, z_recv, d_send, d_recv):
        def z_copy(t, s):
            view = buf.at[away(s), tokens[t]]
            return remote(view, view, z_send.at[t, s], z_recv.at[t, s], to_nxt)

        def d_copy(s, t=None):
            view = buf.at[away(s)] if t is None else buf.at[away(s), tokens[t]]
            slot = s if t is None else s + t
            return remote(view, view, d_send.at[slot], d_recv.at[slot], to_sib)

        return z_copy, d_copy

    def pass_on(z_copy, d_copy, filler):
        def turn(s, carry):
            for t in all_tokens:
                z_copy(t, s - 1).wait_recv()
                z_copy(t, s).start()
            d_copy(s).start()
            filler(s)
            return carry

        lax.fori_loop(1, 7, turn, 0)
        for t in all_tokens:
            z_copy(t, 6).wait_recv()
            pl.when(is_far)(lambda: z_copy(t, 7).start())
        d_copy(7).start()

    def collect(z_copy, d_copy):
        @pl.when(is_far)
        def _():
            for t in all_tokens:
                z_copy(t, 7).wait_recv()
                d_copy(8, t).start()

        for s in range(1, 8):
            d_copy(s).wait_recv()

        @pl.when(is_near)
        def _():
            for t in all_tokens:
                d_copy(8, t).wait_recv()

    a_copy, ad_copy = ring(w_all, a_send, a_recv, ad_send, ad_recv)
    u_copy, ud_copy = ring(u_all, u_send, u_recv, ud_send, ud_recv)

    halo = (
        remote(kcat.at[pl.ds(WINDOW, TOK)], kcat.at[pl.ds(0, WINDOW)], halo_send.at[0], halo_recv.at[0], {"context": following}),
        remote(vcat.at[pl.ds(WINDOW, TOK)], vcat.at[pl.ds(0, WINDOW)], halo_send.at[1], halo_recv.at[1], {"context": following}),
    )

    for t in all_tokens:
        a_copy(t, 0).start()
    for load in loads:
        load.wait()

    def prepare(b, carry):
        r = pl.ds(pl.multiple_of(b * 64, 64), 64)
        near = pl.ds(pl.multiple_of(b * 64 + WINDOW, 64), 64)
        k = kcat[near, :].astype(F32)
        fk[r, :] = (k * lax.rsqrt(jnp.mean(k * k, axis=-1, keepdims=True) + 1e-06)).astype(BF16)
        x = qs[r, :].astype(F32)
        fq[r, :] = (x * lax.rsqrt(jnp.mean(x * x, axis=-1, keepdims=True) + 1e-06)).astype(BF16)
        return carry

    lax.fori_loop(0, 8, prepare, 0)
    for b in range(TOK // 128):
        step = jnp.transpose(jnp.broadcast_to(step_ref[b : b + 1, :], (128, 128)))[:, 0:1]
        near = pl.ds(b * 128 + WINDOW, 128)
        tgt[b * 128 : b * 128 + 128, :] = (-(step * vcat[near, :].astype(F32))).astype(BF16)

    pass_on(a_copy, ad_copy, lambda s: None)
    for copy in halo:
        copy.start()
    collect(a_copy, ad_copy)

    def whole(buf, m):
        return buf[:, units[m]].reshape(FD, FD)

    def g_copy(m, s):
        return remote(
            grad.at[around(sg * (s - 8)), units[m]], grad_sib.at[s, units[m]],
            g_send.at[m, s], g_recv.at[m, s], to_sib,
        )

    def local(t, s):
        return grad[around(sg * (8 - s)), tokens[t]].astype(F32) + grad_sib[s, tokens[t]].astype(F32)

    def r_copy(t, s):
        return remote(run.at[s, tokens[t]], run.at[s + 1, tokens[t]], r_send.at[t, s], r_recv.at[t, s], to_nxt)

    def gradient(m, a, b):
        full = dot(a[...], b[...], TN).astype(BF16).reshape(NZ, 3, 16, FD)
        for k in range(NZ):
            grad[around(k - z), units[m]] = full[k]
        pl.when(is_near)(lambda: g_copy(m, 0).start())
        for s in range(1, 8):
            g_copy(m, s).start()

    def begin(first, last):
        for s, here in ((0, is_far), (1, is_near)):

            @pl.when(here)
            def _():
                for t in range(first, last):
                    if t in FIRST_OF:
                        g_copy(FIRST_OF[t], s).wait_recv()
                    run[s, tokens[t]] = local(t, s).astype(BF16)
                    r_copy(t, s).start()

    gate = dot(fk[...], whole(w_all, 1), NN)
    up = dot(fk[...], whole(w_all, 2), NN)
    sg_gate = jax.nn.sigmoid(gate)
    hid[...] = (gate * sg_gate * up).astype(BF16)
    gradient(0, tgt, hid)
    back = dot(tgt[...], whole(w_all, 0), NT)
    d_gate[...] = (back * up * sg_gate * (1.0 + gate * (1.0 - sg_gate))).astype(BF16)
    d_up[...] = (back * gate * sg_gate).astype(BF16)
    begin(0, 1)
    gradient(1, d_gate, fk)
    gradient(2, d_up, fk)
    begin(1, 5)

    pick = (
        lax.broadcasted_iota(jnp.int32, (SLAB, FD), 1)
        == lax.broadcasted_iota(jnp.int32, (SLAB, FD), 0) + z * SLAB
    ).astype(BF16)
    for m in range(3):
        w_t[m] = dot(pick, whole(w_all, m), NT)

    def reduce_step(t, s):
        r_copy(t, s - 1).wait_recv()
        if t in FIRST_OF:
            g_copy(FIRST_OF[t], s).wait_recv()
        run[s, tokens[t]] = (run[s, tokens[t]].astype(F32) + local(t, s)).astype(BF16)
        r_copy(t, s).start()

    @pl.when(is_far)
    def _():
        for t in all_tokens:
            reduce_step(t, 1)

    def reduce_turn(s, carry):
        for t in all_tokens:
            reduce_step(t, s)
        return carry

    lax.fori_loop(2, 8, reduce_turn, 0)

    def f_copy(m):
        return remote(last_mine.at[units[m]], last_sib.at[units[m]], f_send.at[m], f_recv.at[m], to_sib)

    for m, ready in enumerate(((0, 1), (2,), (3, 4))):
        for t in ready:
            r_copy(t, 7).wait_recv()
        last_mine[units[m]] = (run[8, units[m]].astype(F32) + grad[0, units[m]].astype(F32)).astype(BF16)
        f_copy(m).start()

    for m, ready in enumerate(((0,), (1, 2), (3, 4))):
        old = w_t[m]
        old_ms = jnp.mean(old * old, axis=1, keepdims=True)
        f_copy(m).wait_recv()
        total = last_mine[units[m]].astype(F32) + last_sib[units[m]].astype(F32)
        new = old - total.reshape(SLAB, FD)
        new_ms = jnp.mean(new * new, axis=1, keepdims=True)
        u_all[z, units[m]] = (new * (jnp.sqrt(old_ms) * lax.rsqrt(new_ms + 1e-06))).astype(BF16).reshape(3, 16, FD)
        for t in ready:
            u_copy(t, 0).start()

    for copy in halo:
        copy.wait_recv()
    low_limit = jnp.where(c == 0, WINDOW, 0)

    def attend(piece):
        h = lax.div(piece, 4)
        first = pl.multiple_of(lax.rem(piece, 4) * 128, 128)
        cols = pl.ds(pl.multiple_of(h * HD, HD), HD)
        kb = kcat[pl.ds(first, 640), cols]
        vb = vcat[pl.ds(first, 640), cols]
        scores = dot(qs[pl.ds(first, 128), cols], kb, NT) * (1.0 / math.sqrt(HD))
        t = lax.broadcasted_iota(jnp.int32, (128, 640), 0)
        j = lax.broadcasted_iota(jnp.int32, (128, 640), 1)
        allowed = (j > t) & (j <= t + WINDOW) & (j + first >= low_limit)
        scores = jnp.where(allowed, scores, -1e30)
        powers = jnp.exp(scores - jnp.max(scores, axis=-1, keepdims=True))
        total = jnp.sum(powers, axis=-1, keepdims=True)
        out[0, pl.ds(first, 128), cols] = (dot(powers.astype(BF16), vb, NN) / total).astype(BF16)

    def attend_some(s):
        for k in range(3):
            attend(3 * s + k)

    attend_some(0)
    pass_on(u_copy, ud_copy, attend_some)
    attend_some(7)
    collect(u_copy, ud_copy)

    gate = dot(fq[...], whole(u_all, 1), NT)
    up = dot(fq[...], whole(u_all, 2), NT)
    hid[...] = (gate * jax.nn.sigmoid(gate) * up).astype(BF16)
    out[1] = dot(hid[...], whole(u_all, 0), NT).astype(BF16)

    def sent(s, carry):
        ad_copy(s + 1).wait_send()
        ud_copy(s + 1).wait_send()
        for t in all_tokens:
            a_copy(t, s).wait_send()
            r_copy(t, s + 1).wait_send()
            u_copy(t, s).wait_send()
        return carry

    lax.fori_loop(0, 7, sent, 0)

    @pl.when(is_far)
    def _():
        for t in all_tokens:
            ad_copy(8, t).wait_send()
            ud_copy(8, t).wait_send()
            a_copy(t, 7).wait_send()
            r_copy(t, 0).wait_send()
            u_copy(t, 7).wait_send()

    for m in range(3):
        pl.when(is_near)(lambda: g_copy(m, 0).wait_send())
        for s in range(1, 8):
            g_copy(m, s).wait_send()
        f_copy(m).wait_send()
    for copy in halo:
        copy.wait_send()


def body(query_rows, key_rows, value_rows, step_sizes, w_gate, w_up, w_down):
    dma = pltpu.SemaphoreType.DMA
    vmem = pltpu.VMEM
    anywhere = pl.BlockSpec(memory_space=pl.ANY)
    inside = pl.BlockSpec(memory_space=pltpu.VMEM)
    slabs = (NZ, UNITS, 16, FD)
    out = pl.pallas_call(
        kernel,
        out_shape=jax.ShapeDtypeStruct((2, TOK, FD), BF16),
        in_specs=[anywhere] * 3 + [inside] * 4,
        out_specs=inside,
        scratch_shapes=[
            vmem((TOK, FD), BF16),
            vmem((TOK + WINDOW, FD), BF16),
            vmem((TOK + WINDOW, FD), BF16),
            vmem((TOK, FD), BF16),
            vmem((TOK, FD), BF16),
            vmem((TOK, FD), BF16),
            vmem((3, 32, FD), BF16),
            vmem((3, 32, FD), BF16),
            vmem(slabs, BF16),
            vmem(slabs, BF16),
            vmem((8, UNITS, 16, FD), BF16),
            vmem((9, UNITS, 16, FD), BF16),
            vmem((3, SLAB, FD), F32),
            vmem((UNITS, 16, FD), BF16),
            vmem((UNITS, 16, FD), BF16),
            vmem(slabs, BF16),
            vmem((TOK, FD), BF16),
            vmem((TOK, FD), BF16),
            vmem((TOK, FD), BF16),
            dma((3,)), dma((2,)), dma((2,)), dma, dma,
            dma((5, 8)), dma((5, 8)), dma((13,)), dma((13,)),
            dma((3, 8)), dma((3, 8)), dma((5, 8)), dma((5, 8)), dma((3,)), dma((3,)),
            dma((5, 8)), dma((5, 8)), dma((13,)), dma((13,)),
        ],
        compiler_params=pltpu.CompilerParams(
            collective_id=0, has_side_effects=True, vmem_limit_bytes=56 * 2**20
        ),
        cost_estimate=pl.CostEstimate(flops=7 * 10**9, bytes_accessed=5 * 10**6, transcendentals=4 * 10**6),
        name="attend_and_update",
    )(query_rows, key_rows, value_rows, step_sizes.reshape(TOK // 128, 128), w_gate, w_up, w_down)
    return out[0], out[1]


def solution(mesh):
    tokens = P(("seqs", "context"), "fheads")
    weights = P("fheads", "context", None)
    return jax.shard_map(
        body,
        mesh=mesh,
        in_specs=(tokens,) * 4 + (weights,) * 3,
        out_specs=(tokens, tokens),
        check_vma=False,
    )
```
